256 devices in a mesh: row: 16 (over z_hi, y), col: 16 (over z_lo, x, core).
Axes of the slice: x: 4, y: 4, z: 8 (z_hi: 4, z_lo: 2; z = z_hi * 2 + z_lo), core: 2. Of those that a mesh axis runs over, the one named last changes fastest.
Arguments:
- iterate: bfloat16 [7168, 10240], P('row', 'col'), may hold values from -0.03125 to 0.03125
Outputs:
- update: bfloat16 [7168, 10240], P('row', 'col')
The draws below stay inside these ranges and needn't reach their ends.
All inputs are finite; a program needn't handle non-finite values.
Results may differ from the reference program's by a relative error of at most 0.017.
Values may be sent and summed in bfloat16 or wider, within the bound.
A program may use at most 128 MiB of HBM per device.

```python
import math
import jax
import jax.numpy as jnp
from jax import lax

M = 7168
N = 10240
COLS_DEV = 640
N_COL = 16


def block_levels(rng, dims, cuts, smallest, top_value):
    factor_of, own = 1.0, jax.random.fold_in(rng, 6)
    for position, blocks in cuts:
        steps = jnp.exp(jax.random.uniform(jax.random.fold_in(own, position), (blocks,), jnp.float32, smallest / len(cuts), top_value / len(cuts)))
        factor_of = factor_of * jnp.repeat(steps, dims[position] // blocks).reshape([-1 if axis == position else 1 for axis in range(len(dims))])
    return factor_of


def gaussian(own_key, dims, spread, most, cuts=(), dtype=jnp.bfloat16):
    array = jax.random.normal(own_key, dims, jnp.float32) * spread
    if len(cuts) > 0:
        array = block_levels(own_key, dims, cuts, -0.22, 0.18) * array
    return jnp.clip(array, min=-most, max=most).astype(dtype)


def setup_inputs(seed: int = 0) -> dict:
    arg_keys = jax.random.split(jax.random.key(seed), 2)
    iterate = gaussian(arg_keys[0], (M, N), (4 * N) ** -0.5, 0.03125, ((0, 16), (1, 16)))
    return dict(iterate=iterate)


def reference(iterate):
    gram_sum = jnp.zeros((M, M), jnp.float32)
    for block in range(N_COL):
        cols = iterate[:, block * COLS_DEV:(block + 1) * COLS_DEV]
        partial_c = jnp.dot(cols, cols.T, preferred_element_type=jnp.float32).astype(jnp.bfloat16)
        partial_c = lax.optimization_barrier(partial_c)
        gram_sum = gram_sum + partial_c.astype(jnp.float32)
    gram = gram_sum.astype(jnp.bfloat16)
    applied = jnp.dot(gram, iterate, preferred_element_type=jnp.float32)
    applied_round = applied.astype(jnp.bfloat16)
    twice = jnp.dot(gram, applied_round, preferred_element_type=jnp.float32)
    total = 3.4445 * iterate.astype(jnp.float32) - 4.775 * applied + 2.0315 * twice
    return (math.sqrt(N) * total).astype(jnp.bfloat16)
```

```python
import math

import jax
import jax.numpy as jnp
from jax import lax
from jax.sharding import Mesh, PartitionSpec as P

N = 10240
F32 = jnp.float32
BF16 = jnp.bfloat16


def local(iterate):
    rows_i = lax.all_gather(iterate, "y", axis=0, tiled=True)
    rows_j = lax.all_gather(iterate, "zh", axis=0, tiled=True)
    part = lax.dot_general(
        rows_i, rows_j, (((1,), (1,)), ((), ())), preferred_element_type=F32
    ).astype(BF16)
    piece = lax.psum_scatter(part, ("zl", "x", "core"), scatter_dimension=0, tiled=True)
    gram = lax.all_gather(piece, ("zl", "x", "core"), axis=0, tiled=True)

    def apply(right):
        out = jnp.dot(gram, right, preferred_element_type=F32).astype(BF16)
        return lax.psum_scatter(out, "y", scatter_dimension=0, tiled=True)

    applied = apply(rows_j)
    twice = apply(lax.all_gather(applied, "zh", axis=0, tiled=True))
    total = (
        3.4445 * iterate.astype(F32)
        - 4.775 * applied.astype(F32)
        + 2.0315 * twice.astype(F32)
    )
    return (math.sqrt(N) * total).astype(BF16)


def solution(mesh):
    fine = Mesh(mesh.devices.reshape(4, 4, 2, 4, 2), ("zh", "y", "zl", "x", "core"))
    spec = P(("zh", "y"), ("zl", "x", "core"))
    return jax.shard_map(local, mesh=fine, in_specs=(spec,), out_specs=spec, check_vma=False)
```

```python
import functools
import math

import jax
import jax.numpy as jnp
from jax import lax
from jax.experimental import pallas as pl
from jax.experimental.pallas import tpu as pltpu
from jax.sharding import Mesh, PartitionSpec as P

F32 = jnp.float32
BF16 = jnp.bfloat16
MESH = pl.DeviceIdType.MESH

N = 10240
R = 448
C = 640
J_CUTS = ((0, 384), (384, 512), (896, 384), (1280, 512))
C_CUTS = ((0, 256), (256, 256), (512, 128))
SIZE = {"zh": 4, "y": 4, "zl": 2, "x": 4, "core": 2}
PEERS = (("y", 1), ("y", -1), ("zh", 1), ("zh", -1), ("x", 1), ("x", -1), ("zl", 1), ("core", 1))
COPIES = 120


def dot_nt(a, b):
    return lax.dot_general(a, b, (((1,), (1,)), ((), ())), preferred_element_type=F32)


def dot(a, b):
    return jnp.dot(a, b, preferred_element_type=F32)


def kernel(
    x_ref, o_ref, rows_i, rows_j, gram, half_out, half_in, half, half_f32, rs1, rs2, own_f32, zl_out,
    zl_in, acc, yp, y1, y2, applied, yj, tp, t1, t2, t0, local_sem, send_sem, recv_sem,
):
    where = {name: lax.axis_index(name) for name in SIZE}
    core, x, zl = where["core"], where["x"], where["zl"]
    peer = {
        (name, step): {name: lax.rem(where[name] + step + SIZE[name], SIZE[name])}
        for name, step in PEERS
    }
    x_left, x_right, x_far = (lax.rem(x + d, 4) for d in (3, 1, 2))
    sent = []

    def send(src, dst, name, step):
        at = len(sent)
        copy = pltpu.make_async_remote_copy(
            src, dst, send_sem.at[at], recv_sem.at[at],
            device_id=peer[name, step], device_id_type=MESH,
        )
        copy.start()
        sent.append(copy)
        return copy

    local = [
        pltpu.make_async_copy(x_ref, rows_i.at[0], local_sem.at[0]),
        pltpu.make_async_copy(x_ref, rows_j.at[pl.ds(0, R)], local_sem.at[1]),
    ]
    for copy in local:
        copy.start()
    barrier = pltpu.get_barrier_semaphore()
    for name, step in PEERS:
        pl.semaphore_signal(barrier, inc=1, device_id=peer[name, step], device_id_type=MESH)
    pl.semaphore_wait(barrier, len(PEERS))
    for copy in local:
        copy.wait()

    def part(place, side=None):
        if side is None:
            return pl.ds(place * R, R)
        return pl.ds(place * R + side * (R // 2), R // 2)

    def gather_near(buf):
        return (
            send(buf.at[part(0)], buf.at[part(1)], "zh", -1),
            send(buf.at[part(0)], buf.at[part(2)], "zh", 1),
        )

    def gather_far(buf):
        return (
            send(buf.at[part(1, 0)], buf.at[part(3, 0)], "zh", -1),
            send(buf.at[part(2, 1)], buf.at[part(3, 1)], "zh", 1),
        )

    def arrive(copies):
        for copy in copies:
            copy.wait_recv()

    y_near = (
        send(rows_i.at[0], rows_i.at[1], "y", -1),
        send(rows_i.at[0], rows_i.at[2], "y", 1),
    )
    z_near = gather_near(rows_j)
    arrive(y_near)
    lo, hi = pl.ds(0, R // 2), pl.ds(R // 2, R // 2)
    y_far = (
        send(rows_i.at[1, lo], rows_i.at[3, lo], "y", -1),
        send(rows_i.at[2, hi], rows_i.at[3, hi], "y", 1),
    )

    flight = {}

    def products(j):
        if j == 0:
            arrive(y_far)
        elif j == 1:
            arrive(z_near)
            flight["z_far"] = gather_far(rows_j)
        elif j == 3:
            arrive(flight["z_far"])
        start, width = J_CUTS[j]

        def tile(place):
            return dot_nt(rows_i[place], rows_j[pl.ds(start, width)])

        def other(i, carry):
            half_out[j][pl.ds(2 * i, 2)] = tile(2 * (1 - core) + i).astype(BF16).reshape(2, 224, width)
            return carry

        def mine(i, carry):
            half_f32[pl.ds(2 * i, 2), :, :width] = tile(2 * core + i).reshape(2, 224, width)
            return carry

        lax.fori_loop(0, 2, other, 0)
        flight["core", j] = (send(half_out[j], half_in[j], "core", 1),)
        lax.fori_loop(0, 2, mine, 0)

    def pair_sum(j):
        width = J_CUTS[j][1]
        arrive(flight["core", j])

        def add(i, carry):
            half[j][i] = (half_f32[i, :, :width] + half_in[j][i].astype(F32)).astype(BF16)
            return carry

        lax.fori_loop(0, 4, add, 0)
        flight["rs1", j] = (
            send(half[j].at[x_far, pl.ds(0, 112)], rs1[j].at[0], "x", 1),
            send(half[j].at[x_far, pl.ds(112, 112)], rs1[j].at[1], "x", -1),
        )

    def ring_sum(j):
        for side, to, step in ((0, x_right, 1), (1, x_left, -1)):
            arrive(flight["rs1", j][side : side + 1])
            at = pl.ds(112 * side, 112)
            half[j][to, at] = (half[j][to, at].astype(F32) + rs1[j][side].astype(F32)).astype(BF16)
            flight["rs2", j, side] = send(half[j].at[to], rs2[j].at[side], "x", step)

    def own_sum(j):
        width = J_CUTS[j][1]
        arrive((flight["rs2", j, 0], flight["rs2", j, 1]))

        def total(side):
            at = pl.ds(pl.multiple_of(112 * side, 16), 112)
            return half[j][x, at].astype(F32) + rs2[j][0, at].astype(F32) + rs2[j][1, at].astype(F32)

        zl_out[j][...] = total(1 - zl).astype(BF16)
        flight["zl", j] = (send(zl_out[j], zl_in[j], "zl", 1),)
        own_f32[j][...] = total(zl)

    def piece(x_at, zl_at):
        return core * 8 + x_at * 2 + zl_at

    def settle(j):
        arrive(flight["zl", j])
        at = piece(x, zl)
        gram[j][at] = (own_f32[j][...] + zl_in[j][...].astype(F32)).astype(BF16)
        flight["zl_gather", j] = (send(gram[j].at[at], gram[j].at[at], "zl", 1),)

    def share(j, at):
        flight.setdefault(("share", j), []).append(send(at, at, "core", 1))

    def spread(j):
        arrive(flight["zl_gather", j])
        mine = gram[j].at[pl.ds(piece(x, 0), 2)]
        flight["near", j] = (send(mine, mine, "x", 1), send(mine, mine, "x", -1))
        share(j, mine)

    def forward(j):
        arrive(flight["near", j])
        left, right = gram[j].at[piece(x_left, 0)], gram[j].at[piece(x_right, 1)]
        flight["far", j] = (send(left, left, "x", 1), send(right, right, "x", -1))
        share(j, gram[j].at[pl.ds(piece(x_left, 0), 2)])
        share(j, gram[j].at[pl.ds(piece(x_right, 0), 2)])

    def finish(j):
        arrive(flight["far", j])
        share(j, gram[j].at[pl.ds(piece(x_far, 0), 2)])

    def gram_tile(j, place):
        return gram[j][pl.ds(4 * place, 4)].reshape(R, J_CUTS[j][1])

    def apply(j):
        arrive(flight["share", j])
        if j == 3:
            return
        start, width = J_CUTS[j]

        def one(place, carry):
            value = dot(gram_tile(j, place), rows_j[pl.ds(start, width)])
            acc[place] = value if j == 0 else acc[place] + value
            return carry

        lax.fori_loop(0, 4, one, 0)

    stages = (products, pair_sum, ring_sum, own_sum, settle, spread, forward, finish, apply)
    for tick in range(len(stages) + 3):
        for j in range(4):
            if 0 <= tick - j < len(stages):
                stages[tick - j](j)

    def scatter_far(buf, land):
        return (
            send(buf.at[2, lo], land.at[0], "y", 1),
            send(buf.at[2, hi], land.at[1], "y", -1),
        )

    def scatter_near(buf, land, landed, copies):
        out = []
        for side, at, to, step in ((0, lo, 0, 1), (1, hi, 1, -1)):
            arrive(copies[side : side + 1])
            buf[to, at] = (buf[to, at].astype(F32) + land[side].astype(F32)).astype(BF16)
            out.append(send(buf.at[to], landed.at[side], "y", step))
        return out

    def first(c):
        at, width = C_CUTS[c]
        cols = pl.ds(at, width)
        start, depth = J_CUTS[3]

        def value(place):
            return acc[place, :, cols] + dot(gram_tile(3, place), rows_j[pl.ds(start, depth), cols])

        yp[c][2] = value(3).astype(BF16)
        flight["y1", c] = scatter_far(yp[c], y1[c])
        yp[c][0] = value(1).astype(BF16)
        yp[c][1] = value(2).astype(BF16)
        applied[c][...] = value(0)

    def second(c):
        flight["y2", c] = scatter_near(yp[c], y1[c], y2[c], flight["y1", c])

    def third(c):
        arrive(flight["y2", c])
        value = applied[c][...] + y2[c][0].astype(F32) + y2[c][1].astype(F32)
        yj[c][pl.ds(0, R)] = value.astype(BF16)
        flight["yz", c] = gather_near(yj[c])
        applied[c][...] = value

    def fourth(c):
        arrive(flight["yz", c])
        flight["yf", c] = gather_far(yj[c])

    def fifth(c):
        arrive(flight["yf", c])

        def value(place):
            return sum(
                dot(gram_tile(j, place), yj[c][pl.ds(start, depth)])
                for j, (start, depth) in enumerate(J_CUTS)
            )

        tp[c][2] = value(3).astype(BF16)
        flight["t1", c] = scatter_far(tp[c], t1[c])
        tp[c][0] = value(1).astype(BF16)
        tp[c][1] = value(2).astype(BF16)
        t0[c][...] = value(0)

    def sixth(c):
        flight["t2", c] = scatter_near(tp[c], t1[c], t2[c], flight["t1", c])

    def seventh(c):
        arrive(flight["t2", c])
        at, width = C_CUTS[c]
        cols = pl.ds(at, width)
        twice = t0[c][...] + t2[c][0].astype(F32) + t2[c][1].astype(F32)
        total = 3.4445 * rows_i[0, :, cols].astype(F32) - 4.775 * applied[c][...] + 2.0315 * twice
        o_ref[:, cols] = (math.sqrt(N) * total).astype(BF16)

    steps = (first, second, third, fourth, fifth, sixth, seventh)
    for tick in range(len(steps) + 2):
        for c in range(3):
            if 0 <= tick - c < len(steps):
                steps[tick - c](c)

    for copy in sent:
        copy.wait_send()


def local(iterate):
    def per_chunk(*shape, dtype=BF16):
        return [pltpu.VMEM((*shape, width), dtype) for _, width in J_CUTS]

    def per_cut(*shape, dtype=BF16):
        return [pltpu.VMEM((*shape, width), dtype) for _, width in C_CUTS]

    scratch = dict(
        rows_i=pltpu.VMEM((4, R, C), BF16),
        rows_j=pltpu.VMEM((4 * R, C), BF16),
        gram=per_chunk(16, 112),
        half_out=per_chunk(4, 224),
        half_in=per_chunk(4, 224),
        half=per_chunk(4, 224),
        half_f32=pltpu.VMEM((4, 224, 512), F32),
        rs1=per_chunk(2, 112),
        rs2=per_chunk(2, 224),
        own_f32=per_chunk(112, dtype=F32),
        zl_out=per_chunk(112),
        zl_in=per_chunk(112),
        acc=pltpu.VMEM((4, R, C), F32),
        yp=per_cut(3, R),
        y1=per_cut(2, R // 2),
        y2=per_cut(2, R),
        applied=per_cut(R, dtype=F32),
        yj=per_cut(4 * R),
        tp=per_cut(3, R),
        t1=per_cut(2, R // 2),
        t2=per_cut(2, R),
        t0=per_cut(R, dtype=F32),
        local_sem=pltpu.SemaphoreType.DMA((2,)),
        send_sem=pltpu.SemaphoreType.DMA((COPIES,)),
        recv_sem=pltpu.SemaphoreType.DMA((COPIES,)),
    )
    return pl.pallas_call(
        kernel,
        out_shape=jax.ShapeDtypeStruct((R, C), BF16),
        in_specs=[pl.BlockSpec(memory_space=pl.ANY)],
        out_specs=pl.BlockSpec(memory_space=pltpu.VMEM),
        scratch_shapes=scratch,
        compiler_params=pltpu.CompilerParams(
            collective_id=0, has_side_effects=True, vmem_limit_bytes=60 * 2**20
        ),
        cost_estimate=pl.CostEstimate(
            flops=12_600_000_000, bytes_accessed=1_200_000, transcendentals=0
        ),
    )(iterate)


def solution(mesh):
    fine = Mesh(mesh.devices.reshape(4, 4, 2, 4, 2), tuple(SIZE))
    spec = P(("zh", "y"), ("zl", "x", "core"))
    return jax.shard_map(local, mesh=fine, in_specs=(spec,), out_specs=spec, check_vma=False)
```

```python
import functools
import math

import jax
import jax.numpy as jnp
from jax import lax
from jax.experimental import pallas as pl
from jax.experimental.pallas import tpu as pltpu
from jax.sharding import Mesh, PartitionSpec as P

F32 = jnp.float32
BF16 = jnp.bfloat16
MESH = pl.DeviceIdType.MESH

N = 10240
R = 448
C = 640
J_CUTS = ((0, 384), (384, 512), (896, 384), (1280, 512))
C_CUTS = ((0, 128), (128, 128), (256, 128), (384, 128), (512, 128))
SIZE = {"zh": 4, "y": 4, "zl": 2, "x": 4, "core": 2}
PEERS = (("y", 1), ("y", -1), ("zh", 1), ("zh", -1), ("x", 1), ("x", -1), ("zl", 1), ("core", 1))
COPIES = 160
READY = (27, 38, 40, 53)
STEP = 7
TIMES = (0, 3, 6, 16, 23, 27, 31)
PACE = (2, 2, 2.5, 6, 7, 7, 7)


def dot_nt(a, b):
    return lax.dot_general(a, b, (((1,), (1,)), ((), ())), preferred_element_type=F32)


def dot(a, b):
    return jnp.dot(a, b, preferred_element_type=F32)


def kernel(
    x_ref, o_ref, rows_i, rows_j, gram, half_out, half_in, half, half_f32, rs1, rs2, own_f32, zl_out,
    zl_in, acc, yp, y1, y2, applied, yj, tp, t1, t2, t0, local_sem, send_sem, recv_sem,
):
    where = {name: lax.axis_index(name) for name in SIZE}
    core, x, zl = where["core"], where["x"], where["zl"]
    peer = {
        (name, step): {name: lax.rem(where[name] + step + SIZE[name], SIZE[name])}
        for name, step in PEERS
    }
    x_left, x_right, x_far = (lax.rem(x + d, 4) for d in (3, 1, 2))
    sent = []

    def send(src, dst, name, step):
        at = len(sent)
        copy = pltpu.make_async_remote_copy(
            src, dst, send_sem.at[at], recv_sem.at[at],
            device_id=peer[name, step], device_id_type=MESH,
        )
        copy.start()
        sent.append(copy)
        return copy

    local = [
        pltpu.make_async_copy(x_ref, rows_i.at[0], local_sem.at[0]),
        pltpu.make_async_copy(x_ref, rows_j.at[pl.ds(0, R)], local_sem.at[1]),
    ]
    for copy in local:
        copy.start()
    barrier = pltpu.get_barrier_semaphore()
    for name, step in PEERS:
        pl.semaphore_signal(barrier, inc=1, device_id=peer[name, step], device_id_type=MESH)
    pl.semaphore_wait(barrier, len(PEERS))
    for copy in local:
        copy.wait()

    def part(place, side=None):
        if side is None:
            return pl.ds(place * R, R)
        return pl.ds(place * R + side * (R // 2), R // 2)

    def gather_near(buf):
        return (
            send(buf.at[part(0)], buf.at[part(1)], "zh", -1),
            send(buf.at[part(0)], buf.at[part(2)], "zh", 1),
        )

    def gather_far(buf):
        return (
            send(buf.at[part(1, 0)], buf.at[part(3, 0)], "zh", -1),
            send(buf.at[part(2, 1)], buf.at[part(3, 1)], "zh", 1),
        )

    def arrive(copies):
        for copy in copies:
            copy.wait_recv()

    y_near = (
        send(rows_i.at[0], rows_i.at[1], "y", -1),
        send(rows_i.at[0], rows_i.at[2], "y", 1),
    )
    z_near = gather_near(rows_j)
    arrive(y_near)
    lo, hi = pl.ds(0, R // 2), pl.ds(R // 2, R // 2)
    y_far = (
        send(rows_i.at[1, lo], rows_i.at[3, lo], "y", -1),
        send(rows_i.at[2, hi], rows_i.at[3, hi], "y", 1),
    )

    flight = {}

    def products(j):
        if j == 0:
            arrive(y_far)
        elif j == 1:
            arrive(z_near)
            flight["z_far"] = gather_far(rows_j)
        elif j == 3:
            arrive(flight["z_far"])
        start, width = J_CUTS[j]

        def tile(place):
            return dot_nt(rows_i[place], rows_j[pl.ds(start, width)])

        def other(i, carry):
            half_out[j][pl.ds(2 * i, 2)] = tile(2 * (1 - core) + i).astype(BF16).reshape(2, 224, width)
            return carry

        def mine(i, carry):
            half_f32[j][pl.ds(2 * i, 2)] = tile(2 * core + i).reshape(2, 224, width)
            return carry

        lax.fori_loop(0, 2, other, 0)
        flight["core", j] = (send(half_out[j], half_in[j], "core", 1),)
        lax.fori_loop(0, 2, mine, 0)

    def pair_sum(j):
        width = J_CUTS[j][1]
        arrive(flight["core", j])

        def add(i, carry):
            half[j][i] = (half_f32[j][i] + half_in[j][i].astype(F32)).astype(BF16)
            return carry

        lax.fori_loop(0, 4, add, 0)
        flight["rs1", j] = (
            send(half[j].at[x_far, pl.ds(0, 112)], rs1[j].at[0], "x", 1),
            send(half[j].at[x_far, pl.ds(112, 112)], rs1[j].at[1], "x", -1),
        )

    def ring_sum(j):
        for side, to, step in ((0, x_right, 1), (1, x_left, -1)):
            arrive(flight["rs1", j][side : side + 1])
            at = pl.ds(112 * side, 112)
            half[j][to, at] = (half[j][to, at].astype(F32) + rs1[j][side].astype(F32)).astype(BF16)
            flight["rs2", j, side] = send(half[j].at[to], rs2[j].at[side], "x", step)

    def own_sum(j):
        width = J_CUTS[j][1]
        arrive((flight["rs2", j, 0], flight["rs2", j, 1]))

        def total(side):
            at = pl.ds(pl.multiple_of(112 * side, 16), 112)
            return half[j][x, at].astype(F32) + rs2[j][0, at].astype(F32) + rs2[j][1, at].astype(F32)

        zl_out[j][...] = total(1 - zl).astype(BF16)
        flight["zl", j] = (send(zl_out[j], zl_in[j], "zl", 1),)
        own_f32[j][...] = total(zl)

    def piece(x_at, zl_at):
        return core * 8 + x_at * 2 + zl_at

    def settle(j):
        arrive(flight["zl", j])
        at = piece(x, zl)
        gram[j][at] = (own_f32[j][...] + zl_in[j][...].astype(F32)).astype(BF16)
        flight["zl_gather", j] = (send(gram[j].at[at], gram[j].at[at], "zl", 1),)

    def share(j, at):
        flight.setdefault(("share", j), []).append(send(at, at, "core", 1))

    def spread(j):
        arrive(flight["zl_gather", j])
        mine = gram[j].at[pl.ds(piece(x, 0), 2)]
        flight["near", j] = (send(mine, mine, "x", 1), send(mine, mine, "x", -1))
        share(j, mine)

    def forward(j):
        arrive(flight["near", j])
        left, right = gram[j].at[piece(x_left, 0)], gram[j].at[piece(x_right, 1)]
        flight["far", j] = (send(left, left, "x", 1), send(right, right, "x", -1))
        share(j, gram[j].at[pl.ds(piece(x_left, 0), 2)])
        share(j, gram[j].at[pl.ds(piece(x_right, 0), 2)])

    def finish(j):
        arrive(flight["far", j])
        share(j, gram[j].at[pl.ds(piece(x_far, 0), 2)])

    def gram_tile(j, place):
        return gram[j][pl.ds(4 * place, 4)].reshape(R, J_CUTS[j][1])

    def apply(j):
        arrive(flight["share", j])
        if j == 3:
            return
        start, width = J_CUTS[j]

        def one(place, carry):
            value = dot(gram_tile(j, place), rows_j[pl.ds(start, width)])
            acc[place] = value if j == 0 else acc[place] + value
            return carry

        lax.fori_loop(0, 4, one, 0)

    stages = (products, pair_sum, ring_sum, own_sum, settle, spread, forward, finish, apply)
    for _, j, stage in sorted(
        (READY[j] + STEP * stage, j, stage) for j in range(len(J_CUTS)) for stage in range(len(stages))
    ):
        stages[stage](j)

    def scatter_far(buf, land):
        return (
            send(buf.at[2, lo], land.at[0], "y", 1),
            send(buf.at[2, hi], land.at[1], "y", -1),
        )

    def scatter_near(buf, land, landed, copies):
        out = []
        for side, at, to, step in ((0, lo, 0, 1), (1, hi, 1, -1)):
            arrive(copies[side : side + 1])
            buf[to, at] = (buf[to, at].astype(F32) + land[side].astype(F32)).astype(BF16)
            out.append(send(buf.at[to], landed.at[side], "y", step))
        return out

    def first(c):
        at, width = C_CUTS[c]
        cols = pl.ds(at, width)
        start, depth = J_CUTS[3]

        def value(place):
            return acc[place, :, cols] + dot(gram_tile(3, place), rows_j[pl.ds(start, depth), cols])

        yp[c][2] = value(3).astype(BF16)
        flight["y1", c] = scatter_far(yp[c], y1[c])
        yp[c][0] = value(1).astype(BF16)
        yp[c][1] = value(2).astype(BF16)
        applied[c][...] = value(0)

    def second(c):
        flight["y2", c] = scatter_near(yp[c], y1[c], y2[c], flight["y1", c])

    def third(c):
        arrive(flight["y2", c])
        value = applied[c][...] + y2[c][0].astype(F32) + y2[c][1].astype(F32)
        yj[c][pl.ds(0, R)] = value.astype(BF16)
        flight["yz", c] = gather_near(yj[c])
        applied[c][...] = value

    def fourth(c):
        arrive(flight["yz", c])
        flight["yf", c] = gather_far(yj[c])

    def fifth(c):
        arrive(flight["yf", c])

        def value(place):
            return sum(
                dot(gram_tile(j, place), yj[c][pl.ds(start, depth)])
                for j, (start, depth) in enumerate(J_CUTS)
            )

        tp[c][2] = value(3).astype(BF16)
        flight["t1", c] = scatter_far(tp[c], t1[c])
        tp[c][0] = value(1).astype(BF16)
        tp[c][1] = value(2).astype(BF16)
        t0[c][...] = value(0)

    def sixth(c):
        flight["t2", c] = scatter_near(tp[c], t1[c], t2[c], flight["t1", c])

    def seventh(c):
        arrive(flight["t2", c])
        at, width = C_CUTS[c]
        cols = pl.ds(at, width)
        twice = t0[c][...] + t2[c][0].astype(F32) + t2[c][1].astype(F32)
        total = 3.4445 * rows_i[0, :, cols].astype(F32) - 4.775 * applied[c][...] + 2.0315 * twice
        o_ref[:, cols] = (math.sqrt(N) * total).astype(BF16)

    steps = (first, second, third, fourth, fifth, sixth, seventh)
    for _, c, step in sorted(
        (TIMES[step] + PACE[step] * c, c, step) for c in range(len(C_CUTS)) for step in range(len(steps))
    ):
        steps[step](c)

    for copy in sent:
        copy.wait_send()


def local(iterate):
    def per_chunk(*shape, dtype=BF16):
        return [pltpu.VMEM((*shape, width), dtype) for _, width in J_CUTS]

    def per_cut(*shape, dtype=BF16):
        return [pltpu.VMEM((*shape, width), dtype) for _, width in C_CUTS]

    scratch = dict(
        rows_i=pltpu.VMEM((4, R, C), BF16),
        rows_j=pltpu.VMEM((4 * R, C), BF16),
        gram=per_chunk(16, 112),
        half_out=per_chunk(4, 224),
        half_in=per_chunk(4, 224),
        half=per_chunk(4, 224),
        half_f32=per_chunk(4, 224, dtype=F32),
        rs1=per_chunk(2, 112),
        rs2=per_chunk(2, 224),
        own_f32=per_chunk(112, dtype=F32),
        zl_out=per_chunk(112),
        zl_in=per_chunk(112),
        acc=pltpu.VMEM((4, R, C), F32),
        yp=per_cut(3, R),
        y1=per_cut(2, R // 2),
        y2=per_cut(2, R),
        applied=per_cut(R, dtype=F32),
        yj=per_cut(4 * R),
        tp=per_cut(3, R),
        t1=per_cut(2, R // 2),
        t2=per_cut(2, R),
        t0=per_cut(R, dtype=F32),
        local_sem=pltpu.SemaphoreType.DMA((2,)),
        send_sem=pltpu.SemaphoreType.DMA((COPIES,)),
        recv_sem=pltpu.SemaphoreType.DMA((COPIES,)),
    )
    return pl.pallas_call(
        kernel,
        out_shape=jax.ShapeDtypeStruct((R, C), BF16),
        in_specs=[pl.BlockSpec(memory_space=pl.ANY)],
        out_specs=pl.BlockSpec(memory_space=pltpu.VMEM),
        scratch_shapes=scratch,
        compiler_params=pltpu.CompilerParams(
            collective_id=0, has_side_effects=True, vmem_limit_bytes=60 * 2**20
        ),
        cost_estimate=pl.CostEstimate(
            flops=12_600_000_000, bytes_accessed=1_200_000, transcendentals=0
        ),
    )(iterate)


def solution(mesh):
    fine = Mesh(mesh.devices.reshape(4, 4, 2, 4, 2), tuple(SIZE))
    spec = P(("zh", "y"), ("zl", "x", "core"))
    return jax.shard_map(local, mesh=fine, in_specs=(spec,), out_specs=spec, check_vma=False)
```

```python
import functools
import math

import jax
import jax.numpy as jnp
from jax import lax
from jax.experimental import pallas as pl
from jax.experimental.pallas import tpu as pltpu
from jax.sharding import Mesh, PartitionSpec as P

F32 = jnp.float32
BF16 = jnp.bfloat16
MESH = pl.DeviceIdType.MESH

N = 10240
R = 448
C = 640
J_CUTS = ((0, 384), (384, 512), (896, 384), (1280, 512))
C_CUTS = ((0, 128), (128, 128), (256, 128), (384, 128), (512, 128))
SIZE = {"zh": 4, "y": 4, "zl": 2, "x": 4, "core": 2}
PEERS = (("y", 1), ("y", -1), ("zh", 1), ("zh", -1), ("x", 1), ("x", -1), ("zl", 1), ("core", 1))
COPIES = 160
PAIR_FIRST = (2,)
TOP, LOW = pl.ds(0, 64), pl.ds(64, 48)
READY = (27, 38, 40, 53)
STEP = 7
TIMES = (0, 3, 6, 16, 23, 27, 31)
PACE = (2, 2, 2.5, 6, 7, 7, 7)


def dot_nt(a, b):
    return lax.dot_general(a, b, (((1,), (1,)), ((), ())), preferred_element_type=F32)


def dot(a, b):
    return jnp.dot(a, b, preferred_element_type=F32)


def kernel(
    x_ref, o_ref, rows_i, rows_j, gram, half_out, half_in, half, half_f32, rs1, rs2, own_f32, zl_out,
    zl_in, pair_in, pair, acc, yp, y1, y2, applied, yj, tp, t1, t2, t0, local_sem, send_sem, recv_sem,
):
    where = {name: lax.axis_index(name) for name in SIZE}
    core, x, zl = where["core"], where["x"], where["zl"]
    peer = {
        (name, step): {name: lax.rem(where[name] + step + SIZE[name], SIZE[name])}
        for name, step in PEERS
    }
    x_left, x_right, x_far = (lax.rem(x + d, 4) for d in (3, 1, 2))
    sent = []

    def send(src, dst, name, step):
        at = len(sent)
        copy = pltpu.make_async_remote_copy(
            src, dst, send_sem.at[at], recv_sem.at[at],
            device_id=peer[name, step], device_id_type=MESH,
        )
        copy.start()
        sent.append(copy)
        return copy

    local = [
        pltpu.make_async_copy(x_ref, rows_i.at[0], local_sem.at[0]),
        pltpu.make_async_copy(x_ref, rows_j.at[pl.ds(0, R)], local_sem.at[1]),
    ]
    for copy in local:
        copy.start()
    barrier = pltpu.get_barrier_semaphore()
    for name, step in PEERS:
        pl.semaphore_signal(barrier, inc=1, device_id=peer[name, step], device_id_type=MESH)
    pl.semaphore_wait(barrier, len(PEERS))
    for copy in local:
        copy.wait()

    def part(place, side=None):
        if side is None:
            return pl.ds(place * R, R)
        return pl.ds(place * R + side * (R // 2), R // 2)

    def gather_near(buf):
        return (
            send(buf.at[part(0)], buf.at[part(1)], "zh", -1),
            send(buf.at[part(0)], buf.at[part(2)], "zh", 1),
        )

    def gather_far(buf):
        return (
            send(buf.at[part(1, 0)], buf.at[part(3, 0)], "zh", -1),
            send(buf.at[part(2, 1)], buf.at[part(3, 1)], "zh", 1),
        )

    def arrive(copies):
        for copy in copies:
            copy.wait_recv()

    y_near = (
        send(rows_i.at[0], rows_i.at[1], "y", -1),
        send(rows_i.at[0], rows_i.at[2], "y", 1),
    )
    z_near = gather_near(rows_j)
    arrive(y_near)
    lo, hi = pl.ds(0, R // 2), pl.ds(R // 2, R // 2)
    y_far = (
        send(rows_i.at[1, lo], rows_i.at[3, lo], "y", -1),
        send(rows_i.at[2, hi], rows_i.at[3, hi], "y", 1),
    )

    flight = {}

    def products(j):
        if j == 0:
            arrive(y_far)
        elif j == 1:
            arrive(z_near)
            flight["z_far"] = gather_far(rows_j)
        elif j == 3:
            arrive(flight["z_far"])
        start, width = J_CUTS[j]

        def tile(place):
            return dot_nt(rows_i[place], rows_j[pl.ds(start, width)])

        def other(i, carry):
            half_out[j][pl.ds(2 * i, 2)] = tile(2 * (1 - core) + i).astype(BF16).reshape(2, 224, width)
            return carry

        def mine(i, carry):
            half_f32[j][pl.ds(2 * i, 2)] = tile(2 * core + i).reshape(2, 224, width)
            return carry

        lax.fori_loop(0, 2, other, 0)
        flight["core", j] = (send(half_out[j], half_in[j], "core", 1),)
        lax.fori_loop(0, 2, mine, 0)

    def pair_sum(j):
        width = J_CUTS[j][1]
        arrive(flight["core", j])

        def add(i, carry):
            half[j][i] = (half_f32[j][i] + half_in[j][i].astype(F32)).astype(BF16)
            return carry

        lax.fori_loop(0, 4, add, 0)
        if j in PAIR_FIRST:
            theirs = pl.ds(pl.multiple_of(112 * (1 - zl), 16), 112)
            flight["zl", j] = (send(half[j].at[:, theirs], pair_in[j], "zl", 1),)
            return
        flight["rs1", j] = (
            send(half[j].at[x_far, pl.ds(0, 112)], rs1[j].at[0], "x", 1),
            send(half[j].at[x_far, pl.ds(112, 112)], rs1[j].at[1], "x", -1),
        )

    def ring_sum(j):
        for side, to, step in ((0, x_right, 1), (1, x_left, -1)):
            arrive(flight["rs1", j][side : side + 1])
            at = pl.ds(112 * side, 112)
            half[j][to, at] = (half[j][to, at].astype(F32) + rs1[j][side].astype(F32)).astype(BF16)
            flight["rs2", j, side] = send(half[j].at[to], rs2[j].at[side], "x", step)

    def own_sum(j):
        width = J_CUTS[j][1]
        arrive((flight["rs2", j, 0], flight["rs2", j, 1]))

        def total(side):
            at = pl.ds(pl.multiple_of(112 * side, 16), 112)
            return half[j][x, at].astype(F32) + rs2[j][0, at].astype(F32) + rs2[j][1, at].astype(F32)

        zl_out[j][...] = total(1 - zl).astype(BF16)
        flight["zl", j] = (send(zl_out[j], zl_in[j], "zl", 1),)
        own_f32[j][...] = total(zl)

    def piece(x_at, zl_at):
        return core * 8 + x_at * 2 + zl_at

    def settle(j):
        arrive(flight["zl", j])
        at = piece(x, zl)
        gram[j][at] = (own_f32[j][...] + zl_in[j][...].astype(F32)).astype(BF16)
        flight["zl_gather", j] = (send(gram[j].at[at], gram[j].at[at], "zl", 1),)

    def share(j, at):
        flight.setdefault(("share", j), []).append(send(at, at, "core", 1))

    def spread(j):
        arrive(flight["zl_gather", j])
        mine = gram[j].at[pl.ds(piece(x, 0), 2)]
        flight["near", j] = (send(mine, mine, "x", 1), send(mine, mine, "x", -1))
        share(j, mine)

    def forward(j):
        arrive(flight["near", j])
        left, right = gram[j].at[piece(x_left, 0)], gram[j].at[piece(x_right, 1)]
        flight["far", j] = (send(left, left, "x", 1), send(right, right, "x", -1))
        share(j, gram[j].at[pl.ds(piece(x_left, 0), 2)])
        share(j, gram[j].at[pl.ds(piece(x_right, 0), 2)])

    def finish(j):
        arrive(flight["far", j])
        share(j, gram[j].at[pl.ds(piece(x_far, 0), 2)])

    def gram_tile(j, place):
        return gram[j][pl.ds(4 * place, 4)].reshape(R, J_CUTS[j][1])

    def apply(j):
        arrive(flight["share", j])
        if j == 3:
            return
        start, width = J_CUTS[j]

        def one(place, carry):
            value = dot(gram_tile(j, place), rows_j[pl.ds(start, width)])
            acc[place] = value if j == 0 else acc[place] + value
            return carry

        lax.fori_loop(0, 4, one, 0)

    def pair_ring(j):
        arrive(flight["zl", j])
        ours = pl.ds(pl.multiple_of(112 * zl, 16), 112)
        for i in range(4):
            pair[j][i] = (half[j][i, ours].astype(F32) + pair_in[j][i].astype(F32)).astype(BF16)
        flight["rs1", j] = (
            send(pair[j].at[x_far, TOP], rs1[j].at[0, TOP], "x", 1),
            send(pair[j].at[x_far, LOW], rs1[j].at[1, LOW], "x", -1),
        )

    def pair_ring_sum(j):
        for side, to, at, step in ((0, x_right, TOP, 1), (1, x_left, LOW, -1)):
            arrive(flight["rs1", j][side : side + 1])
            pair[j][to, at] = (pair[j][to, at].astype(F32) + rs1[j][side, at].astype(F32)).astype(BF16)
            flight["rs2", j, side] = send(pair[j].at[to], rs2[j].at[side, pl.ds(0, 112)], "x", step)

    def pair_share(j, x_at):
        at = gram[j].at[piece(x_at, zl)]
        flight.setdefault(("pair", j), []).append((x_at, send(at, at, "zl", 1)))
        share(j, at)

    def pair_settle(j):
        arrive((flight["rs2", j, 0], flight["rs2", j, 1]))
        mine = gram[j].at[piece(x, zl)]
        rest = pl.ds(0, 112)
        mine[...] = (
            pair[j][x].astype(F32) + rs2[j][0, rest].astype(F32) + rs2[j][1, rest].astype(F32)
        ).astype(BF16)
        flight["near", j] = (send(mine, mine, "x", 1), send(mine, mine, "x", -1))
        pair_share(j, x)

    def pair_forward(j):
        arrive(flight["near", j])
        left, right = gram[j].at[piece(x_left, zl), TOP], gram[j].at[piece(x_right, zl), LOW]
        flight["far", j] = (send(left, left, "x", 1), send(right, right, "x", -1))
        pair_share(j, x_left)
        pair_share(j, x_right)

    def pair_finish(j):
        arrive(flight["far", j])
        pair_share(j, x_far)

    def pair_spread(j):
        for x_at, copy in flight["pair", j]:
            arrive((copy,))
            share(j, gram[j].at[piece(x_at, 1 - zl)])

    pair_stages = (
        products, pair_sum, pair_ring, pair_ring_sum, pair_settle, pair_forward, pair_finish,
        pair_spread, apply,
    )
    stages = (products, pair_sum, ring_sum, own_sum, settle, spread, forward, finish, apply)
    for _, j, stage in sorted(
        (READY[j] + STEP * stage, j, stage) for j in range(len(J_CUTS)) for stage in range(len(stages))
    ):
        (pair_stages if j in PAIR_FIRST else stages)[stage](j)

    def scatter_far(buf, land):
        return (
            send(buf.at[2, lo], land.at[0], "y", 1),
            send(buf.at[2, hi], land.at[1], "y", -1),
        )

    def scatter_near(buf, land, landed, copies):
        out = []
        for side, at, to, step in ((0, lo, 0, 1), (1, hi, 1, -1)):
            arrive(copies[side : side + 1])
            buf[to, at] = (buf[to, at].astype(F32) + land[side].astype(F32)).astype(BF16)
            out.append(send(buf.at[to], landed.at[side], "y", step))
        return out

    def first(c):
        at, width = C_CUTS[c]
        cols = pl.ds(at, width)
        start, depth = J_CUTS[3]

        def value(place):
            return acc[place, :, cols] + dot(gram_tile(3, place), rows_j[pl.ds(start, depth), cols])

        yp[c][2] = value(3).astype(BF16)
        flight["y1", c] = scatter_far(yp[c], y1[c])
        yp[c][0] = value(1).astype(BF16)
        yp[c][1] = value(2).astype(BF16)
        applied[c][...] = value(0)

    def second(c):
        flight["y2", c] = scatter_near(yp[c], y1[c], y2[c], flight["y1", c])

    def third(c):
        arrive(flight["y2", c])
        value = applied[c][...] + y2[c][0].astype(F32) + y2[c][1].astype(F32)
        yj[c][pl.ds(0, R)] = value.astype(BF16)
        flight["yz", c] = gather_near(yj[c])
        applied[c][...] = value

    def fourth(c):
        arrive(flight["yz", c])
        flight["yf", c] = gather_far(yj[c])

    def fifth(c):
        arrive(flight["yf", c])

        def value(place):
            return sum(
                dot(gram_tile(j, place), yj[c][pl.ds(start, depth)])
                for j, (start, depth) in enumerate(J_CUTS)
            )

        tp[c][2] = value(3).astype(BF16)
        flight["t1", c] = scatter_far(tp[c], t1[c])
        tp[c][0] = value(1).astype(BF16)
        tp[c][1] = value(2).astype(BF16)
        t0[c][...] = value(0)

    def sixth(c):
        flight["t2", c] = scatter_near(tp[c], t1[c], t2[c], flight["t1", c])

    def seventh(c):
        arrive(flight["t2", c])
        at, width = C_CUTS[c]
        cols = pl.ds(at, width)
        twice = t0[c][...] + t2[c][0].astype(F32) + t2[c][1].astype(F32)
        total = 3.4445 * rows_i[0, :, cols].astype(F32) - 4.775 * applied[c][...] + 2.0315 * twice
        o_ref[:, cols] = (math.sqrt(N) * total).astype(BF16)

    steps = (first, second, third, fourth, fifth, sixth, seventh)
    for _, c, step in sorted(
        (TIMES[step] + PACE[step] * c, c, step) for c in range(len(C_CUTS)) for step in range(len(steps))
    ):
        steps[step](c)

    for copy in sent:
        copy.wait_send()


def local(iterate):
    def per_chunk(*shape, dtype=BF16):
        return [pltpu.VMEM((*shape, width), dtype) for _, width in J_CUTS]

    def per_cut(*shape, dtype=BF16):
        return [pltpu.VMEM((*shape, width), dtype) for _, width in C_CUTS]

    scratch = dict(
        rows_i=pltpu.VMEM((4, R, C), BF16),
        rows_j=pltpu.VMEM((4 * R, C), BF16),
        gram=per_chunk(16, 112),
        half_out=per_chunk(4, 224),
        half_in=per_chunk(4, 224),
        half=per_chunk(4, 224),
        half_f32=per_chunk(4, 224, dtype=F32),
        rs1=per_chunk(2, 112),
        rs2=per_chunk(2, 224),
        own_f32=per_chunk(112, dtype=F32),
        zl_out=per_chunk(112),
        zl_in=per_chunk(112),
        pair_in=per_chunk(4, 112),
        pair=per_chunk(4, 112),
        acc=pltpu.VMEM((4, R, C), F32),
        yp=per_cut(3, R),
        y1=per_cut(2, R // 2),
        y2=per_cut(2, R),
        applied=per_cut(R, dtype=F32),
        yj=per_cut(4 * R),
        tp=per_cut(3, R),
        t1=per_cut(2, R // 2),
        t2=per_cut(2, R),
        t0=per_cut(R, dtype=F32),
        local_sem=pltpu.SemaphoreType.DMA((2,)),
        send_sem=pltpu.SemaphoreType.DMA((COPIES,)),
        recv_sem=pltpu.SemaphoreType.DMA((COPIES,)),
    )
    return pl.pallas_call(
        kernel,
        out_shape=jax.ShapeDtypeStruct((R, C), BF16),
        in_specs=[pl.BlockSpec(memory_space=pl.ANY)],
        out_specs=pl.BlockSpec(memory_space=pltpu.VMEM),
        scratch_shapes=scratch,
        compiler_params=pltpu.CompilerParams(
            collective_id=0, has_side_effects=True, vmem_limit_bytes=60 * 2**20
        ),
        cost_estimate=pl.CostEstimate(
            flops=12_600_000_000, bytes_accessed=1_200_000, transcendentals=0
        ),
    )(iterate)


def solution(mesh):
    fine = Mesh(mesh.devices.reshape(4, 4, 2, 4, 2), tuple(SIZE))
    spec = P(("zh", "y"), ("zl", "x", "core"))
    return jax.shard_map(local, mesh=fine, in_specs=(spec,), out_specs=spec, check_vma=False)
```
